512 devices in a mesh: dp: 8 (over z), seq: 8 (over x, core), enc: 8 (over y).
Axes of the slice: x: 4, y: 8, z: 8, core: 2. Of those that a mesh axis runs over, the one named last changes fastest.
Arguments:
- queries: bfloat16 [32768, 2048], P(('dp', 'seq'), 'enc'), may hold values from -6 to 6
- out_grad: bfloat16 [32768, 2048], P(('dp', 'seq'), 'enc'), may hold values from -96 to 96
- keys: bfloat16 [1024, 128, 2048], P(('dp', 'seq'), None, 'enc'), may hold values from -6 to 6
- values: bfloat16 [1024, 128, 2048], P(('dp', 'seq'), None, 'enc'), may hold values from -6 to 6
- neighbour_ids: int32 [512, 2], P(('dp', 'seq')), may hold values from 0 to 15
- neighbour_place: int32 [64, 16], P(('dp', 'seq')), may hold values from 0 to 15, each once within a row
- kv_weight: bfloat16 [2, 896, 2048], P(None, ('dp', 'seq'), 'enc'), may hold values from -0.125 to 0.125
Outputs:
- queries_grad: bfloat16 [32768, 2048], P(('dp', 'seq'), 'enc')
- encoded_grad: bfloat16 [1024, 128, 896], P(('dp', 'seq', 'enc'))
The draws below stay inside these ranges and needn't reach their ends.
Inputs may be any that keep to these rules, and one draw needn't show every extreme that they name: `neighbour_ids`: numbers of neighbours in the span's own batch group; several slots may name the same one. `neighbour_place`: each row is a permutation; store position p lies on owner p // 2 of the group, at entry p % 2.
All inputs are finite; a program needn't handle non-finite values.
Results may differ from the reference program's by a relative error of at most 0.014.
Values may be sent and summed in bfloat16 or wider, within the bound.
No kernel may reach another device: no remote copies, remote signals or barrier semaphores. Data moves between devices by JAX's collectives and lax.ppermute only.
A program may use at most 64 MiB of HBM per device.

```python
import math
import jax
import jax.numpy as jnp
import numpy as np
from jax import lax

HEADS = 16
HD = 128
DE = 896
SPAN = 64
NBT = 128
NEIGH = 2
CAP = 2
HW = 2048
TOKENS = 32768
SLOTS = 1024
N_DP = 8
N_SEQ = 8
N_ENC = 8


def draw_queries(key, part):
    key = jax.random.fold_in(key, 5)
    values = jnp.clip(jax.random.normal(key, (TOKENS, HW), jnp.float32), -6.0, 6.0)
    return values.astype(jnp.bfloat16)


def draw_keys(key, part):
    key = jax.random.fold_in(key, 9)
    values = jnp.clip(jax.random.normal(key, (SLOTS, NBT, HW), jnp.float32), -6.0, 6.0)
    return values.astype(jnp.bfloat16)


def touch_ends(array, rng, least, high):
    place = [jax.random.randint(jax.random.fold_in(rng, axis), (), 0, length) for axis, length in enumerate(array.shape)]
    widest = array.shape.index(max(array.shape))
    neighbour = place[:widest] + [(place[widest] + 1) % array.shape[widest]] + place[widest + 1:]
    return array.at[tuple(place)].set(least).at[tuple(neighbour)].set(high)


def levels(stream_key, shape, pieces, low, top_value):
    factor_of = 1.0
    for position, shards_of in pieces:
        draws = jax.random.uniform(jax.random.fold_in(jax.random.fold_in(stream_key, 6), position), (shards_of,), jnp.float32, low / len(pieces), top_value / len(pieces))
        factor_of = factor_of * jnp.repeat(jnp.exp(draws), shape[position] // shards_of).reshape((-1,) + (1,) * (len(shape) - 1 - position))
    return factor_of


def cumulative_ranks(amount, slope):
    loads = [(1 << 20) // math.isqrt(grade ** slope) + 1 for grade in range(1, amount + 1)]
    width = 1 + sum(loads) // (1 << 30)
    return np.cumsum(np.array([max(1, weight // width) for weight in loads]))


def ranked(rng, shape, amount, slope):
    table = cumulative_ranks(amount, slope)
    ticket = jax.random.randint(jax.random.fold_in(rng, 1), shape, 0, int(table[amount - 1]))
    grade = jnp.searchsorted(jnp.asarray(table, jnp.int32), ticket, side="right")
    return jax.random.permutation(jax.random.fold_in(rng, 2), amount)[grade].astype(jnp.int32)


def scatter_about(key, dims, scale, reach, split=(), kind=jnp.bfloat16):
    level = levels(key, dims, split, -0.22, 0.18) if split else 1.0
    array = jax.random.normal(key, dims, jnp.float32) * scale * level
    return jnp.minimum(jnp.maximum(array, -reach), reach).astype(kind)


def setup_inputs(seed: int = 0) -> dict:
    streams_of = jax.random.split(jax.random.key(seed), 8)
    queries = draw_queries(jax.random.fold_in(streams_of[7], 71), 0)
    out_grad = scatter_about(streams_of[1], (TOKENS, HW), 16.0, 96.0, ((0, 64), (1, 8)))
    keys = draw_keys(jax.random.fold_in(streams_of[7], 71), 0)
    values = scatter_about(streams_of[3], (SLOTS, NBT, HW), 1.0, 6.0, ((0, 64), (2, 8)))
    neighbour_ids = touch_ends(ranked(streams_of[4], (TOKENS // SPAN, NEIGH), N_ENC * CAP, 2), jax.random.fold_in(streams_of[4], 3), 0, (N_ENC * CAP) - 1).astype(jnp.int32)
    neighbour_place = jax.vmap(lambda own: jax.random.permutation(own, N_ENC * CAP))(jax.random.split(streams_of[5], (N_DP * N_SEQ))).reshape((N_DP * N_SEQ, N_ENC * CAP)).astype(jnp.int32)
    kv_weight = scatter_about(streams_of[6], (2, DE, HW), HW ** -0.5, 0.125, ((1, 64), (2, 8)))
    return {"queries": queries, "out_grad": out_grad, "keys": keys, "values": values, "neighbour_ids": neighbour_ids, "neighbour_place": neighbour_place, "kv_weight": kv_weight}


def attention_back(queries, out_grad, keys, values):
    span_count = queries.shape[0] // SPAN
    factor = 1.0 / math.sqrt(HD)
    query_blocks = queries.reshape(span_count, SPAN, HEADS, HD).astype(jnp.float32)
    grad_blocks = out_grad.reshape(span_count, SPAN, HEADS, HD).astype(jnp.float32)
    key_blocks = keys.reshape(span_count, NEIGH * NBT, HEADS, HD).astype(jnp.float32)
    value_blocks = values.reshape(span_count, NEIGH * NBT, HEADS, HD).astype(jnp.float32)
    scores = jnp.einsum('cqhd,ckhd->chqk', query_blocks, key_blocks) * factor
    row_max = lax.optimization_barrier(jnp.max(scores, axis=-1, keepdims=True))
    exponent = jnp.exp(scores - row_max)
    weights = exponent / lax.optimization_barrier(jnp.sum(exponent, axis=-1, keepdims=True))
    weights_low = lax.optimization_barrier(weights.astype(jnp.bfloat16)).astype(jnp.float32)
    attended = jnp.einsum('chqk,ckhd->cqhd', weights_low, value_blocks)
    delta = lax.optimization_barrier(jnp.sum(attended * grad_blocks, axis=-1))
    delta = jnp.transpose(delta, (0, 2, 1))[..., None]
    weight_grad = jnp.einsum('cqhd,ckhd->chqk', grad_blocks, value_blocks)
    score_grad = weights * (weight_grad - delta)
    score_low = lax.optimization_barrier(score_grad.astype(jnp.bfloat16)).astype(jnp.float32)
    query_grad = jnp.einsum('chqk,ckhd->cqhd', score_low, key_blocks) * factor
    key_grad = jnp.einsum('chqk,cqhd->ckhd', score_low, query_blocks) * factor
    value_grad = jnp.einsum('chqk,cqhd->ckhd', weights_low, grad_blocks)
    query_grad = query_grad.reshape(span_count * SPAN, HW).astype(jnp.bfloat16)
    key_grad = key_grad.reshape(span_count * NEIGH, NBT, HW)
    value_grad = value_grad.reshape(span_count * NEIGH, NBT, HW)
    return (query_grad, key_grad, value_grad)

def neighbour_sums(key_grad, value_grad, group_ids, place_row):
    store_size = place_row.shape[0]
    slot_place = place_row[group_ids.reshape(-1)]
    selector = (jnp.arange(store_size).astype(jnp.int32)[:, None] == slot_place[None, :]).astype(jnp.float32)
    stacked = jnp.stack([key_grad, value_grad])
    sums = jnp.einsum('ps,kstf->kptf', selector, stacked, precision=lax.Precision.HIGHEST)
    return lax.optimization_barrier(sums.astype(jnp.bfloat16))

def project_store(store, kv_weight):
    store_size = store.shape[1]
    group_width = HW // N_ENC
    spread = store.reshape(2, store_size, NBT, N_ENC, group_width).astype(jnp.float32)
    weight_rows = kv_weight.reshape(2, DE, N_ENC, group_width).astype(jnp.float32)
    partial_value = jnp.einsum('kpthf,kdhf->hptd', spread, weight_rows)
    partial_value = lax.optimization_barrier(partial_value.astype(jnp.bfloat16)).astype(jnp.float32)
    return lax.optimization_barrier(jnp.sum(partial_value, axis=0)).astype(jnp.bfloat16)

def reference(queries, out_grad, keys, values, neighbour_ids, neighbour_place, kv_weight):
    groups = N_DP * N_SEQ
    tok_group = queries.shape[0] // groups

    def one_group(inputs):
        group_queries, group_grads, group_keys, group_values, group_ids, place_row = inputs
        query_grad, key_grad, value_grad = attention_back(group_queries, group_grads, group_keys, group_values)
        store = neighbour_sums(key_grad, value_grad, group_ids, place_row)
        return (query_grad, project_store(store, kv_weight))
    stacked_inputs = (queries.reshape(groups, tok_group, HW), out_grad.reshape(groups, tok_group, HW), keys.reshape(groups, -1, NBT, HW), values.reshape(groups, -1, NBT, HW), neighbour_ids.reshape(groups, -1, NEIGH), neighbour_place)
    query_grads, encoded = lax.map(one_group, stacked_inputs)
    return (query_grads.reshape(-1, HW), encoded.reshape(-1, NBT, DE))
```

```python
import math

import jax
import jax.numpy as jnp
from jax import lax
from jax.experimental import pallas as pl
from jax.experimental.pallas import tpu as pltpu
from jax.sharding import Mesh
from jax.sharding import PartitionSpec as P

HD = 128
SPAN = 64
NBT = 128
NEIGH = 2
STEP_SPANS = 2

LOW = jnp.bfloat16
F32 = jnp.float32


def dot_nt(a, b):
    return lax.dot_general(a, b, (((1,), (1,)), ((), ())), preferred_element_type=F32)


def dot_tn(a, b):
    return lax.dot_general(a, b, (((0,), (0,)), ((), ())), preferred_element_type=F32)


def dot_nn(a, b):
    return lax.dot_general(a, b, (((1,), (0,)), ((), ())), preferred_element_type=F32)


def attention_kernel(heads, owners, ids, place, q_ref, g_ref, k_ref, v_ref, dq_ref, store_ref, total):
    step = pl.program_id(0)
    factor = 1.0 / math.sqrt(HD)
    width = heads * HD
    me = lax.axis_index("enc")

    @pl.when(step == 0)
    def _():
        total[...] = jnp.zeros_like(total)

    for s in range(STEP_SPANS):
        span = step * STEP_SPANS + s
        slots = []
        for j in range(NEIGH):
            entry = place[0, ids[span, j]]
            away = jnp.where(me % 2 == 0, entry // 2 - me, me - entry // 2)
            slots.append(lax.rem(away + owners, owners) * 2 + entry % 2)
        for h in range(heads):
            cols = slice(h * HD, (h + 1) * HD)
            rows = slice(s * SPAN, (s + 1) * SPAN)
            q = q_ref[rows, cols]
            g = g_ref[rows, cols]
            k = k_ref[s * NEIGH : (s + 1) * NEIGH, :, cols].reshape(NEIGH * NBT, HD)
            v = v_ref[s * NEIGH : (s + 1) * NEIGH, :, cols].reshape(NEIGH * NBT, HD)
            scores = dot_nt(q, k) * factor
            weight_grad = dot_nt(g, v)
            exponent = jnp.exp(scores - jnp.max(scores, axis=1, keepdims=True))
            weights = exponent * (1.0 / jnp.sum(exponent, axis=1, keepdims=True))
            weights_low = weights.astype(LOW)
            delta = jnp.sum(weights_low.astype(F32) * weight_grad, axis=1, keepdims=True)
            score_low = (weights * (weight_grad - delta)).astype(LOW)
            dq_ref[rows, cols] = (dot_nn(score_low, k) * factor).astype(LOW)
            key_grad = dot_tn(score_low, q)
            value_grad = dot_tn(weights_low, g)
            for j in range(NEIGH):
                part = slice(j * NBT, (j + 1) * NBT)
                total[slots[j], :, cols] += key_grad[part]
                total[slots[j], :, width + h * HD : width + (h + 1) * HD] += value_grad[part]

    @pl.when(step == pl.num_programs(0) - 1)
    def _():
        store_ref[:, :, :width] = (total[:, :, :width] * factor).astype(LOW)
        store_ref[:, :, width:] = total[:, :, width:].astype(LOW)


def attention(queries, out_grad, keys, values, ids, place, owners):
    tokens, width = queries.shape
    slots = keys.shape[0]
    entries = place.shape[1]
    steps = slots // (NEIGH * STEP_SPANS)
    row_spec = pl.BlockSpec((STEP_SPANS * SPAN, width), lambda i: (i, 0))
    slot_spec = pl.BlockSpec((STEP_SPANS * NEIGH, NBT, width), lambda i: (i, 0, 0))
    scalars = pl.BlockSpec(memory_space=pltpu.SMEM)

    def kernel(*refs):
        attention_kernel(width // HD, owners, *refs)

    return pl.pallas_call(
        kernel,
        grid=(steps,),
        in_specs=[scalars, scalars, row_spec, row_spec, slot_spec, slot_spec],
        out_specs=[row_spec, pl.BlockSpec((entries, NBT, 2 * width), lambda i: (0, 0, 0))],
        out_shape=[
            jax.ShapeDtypeStruct((tokens, width), LOW),
            jax.ShapeDtypeStruct((entries, NBT, 2 * width), LOW),
        ],
        scratch_shapes=[pltpu.VMEM((entries, NBT, 2 * width), F32)],
        compiler_params=pltpu.CompilerParams(
            dimension_semantics=("arbitrary",), vmem_limit_bytes=40 * 1024 * 1024
        ),
        cost_estimate=pl.CostEstimate(flops=10**9, bytes_accessed=6 * 10**6, transcendentals=2 * 10**6),
        name="attention_back",
    )(ids, place, queries, out_grad, keys, values)


def gather_rows(mine, dp_count, x_count):
    rows, depth = mine.shape
    sources = dp_count * x_count
    copies = jnp.broadcast_to(mine[None], (sources, rows, depth))
    same = lax.all_to_all(copies, ("dp", "sx"), split_axis=0, concat_axis=0, tiled=True)
    other = lax.ppermute(same, "core", [(0, 1), (1, 0)])
    first = lax.axis_index("core") == 0
    low = jnp.where(first, same, other)
    high = jnp.where(first, other, same)
    return jnp.stack([low, high], axis=1).reshape(sources * 2 * rows, depth)


def add_low(a, b):
    return (a.astype(F32) + b.astype(F32)).astype(LOW)


def local(queries, out_grad, keys, values, neighbour_ids, neighbour_place, kv_weight):
    owners = lax.axis_size("enc")
    dp_count, x_count = lax.axis_size("dp"), lax.axis_size("sx")
    rows = kv_weight.shape[1]
    depth = 2 * kv_weight.shape[2]
    half = owners // 2
    opposite = [(i, (i + half) % owners) for i in range(owners)]
    even = [(i, i ^ 1) for i in range(owners)]
    odd = [(i, (i + 1) % owners if i % 2 else (i - 1) % owners) for i in range(owners)]

    mine = jnp.transpose(kv_weight, (1, 0, 2)).reshape(rows, depth)
    weight = gather_rows(mine, dp_count, x_count)
    query_grad, store = attention(
        queries, out_grad, keys, values, neighbour_ids, neighbour_place, owners
    )
    cap = store.shape[0] // owners
    chunk = cap * NBT

    def raw(j):
        return store[j * cap : (j + 1) * cap].reshape(chunk, depth)

    far_raw = lax.ppermute(raw(half), "enc", opposite)
    far_mine = lax.ppermute(mine, "enc", opposite)
    far_mine, weight = lax.optimization_barrier((far_mine, weight))
    far_weight = gather_rows(far_mine, dp_count, x_count)

    part = {j: dot_nt(raw(j), weight).astype(LOW) for j in range(owners) if j != half}

    def on_even(x):
        return lax.ppermute(x, "enc", even)

    def on_odd(x):
        return lax.ppermute(x, "enc", odd)

    a, b = on_even(part[half - 1]), on_odd(part[half + 1])
    for j in range(half - 2, 0, -1):
        a, b = on_even(add_low(b, part[j])), on_odd(add_low(a, part[owners - j]))
    encoded = (
        dot_nt(far_raw, far_weight)
        + part[0].astype(F32)
        + a.astype(F32)
        + b.astype(F32)
    )
    return (query_grad, encoded.astype(LOW).reshape(cap, NBT, -1))


def solution(mesh):
    devices = mesh.devices
    dp_count, seq_count, enc_count = devices.shape
    split = Mesh(
        devices.reshape(dp_count, seq_count // 2, 2, enc_count), ("dp", "sx", "core", "enc")
    )
    group = ("dp", "sx", "core")
    placed = (
        P(group, "enc"),
        P(group, "enc"),
        P(group, None, "enc"),
        P(group, None, "enc"),
        P(group, None),
        P(group, None),
        P(None, group, "enc"),
    )
    return jax.shard_map(
        local,
        mesh=split,
        in_specs=placed,
        out_specs=(P(group, "enc"), P(("dp", "sx", "core", "enc"), None, None)),
        check_vma=False,
    )
```

```python
import math

import jax
import jax.numpy as jnp
from jax import lax
from jax.experimental import pallas as pl
from jax.experimental.pallas import tpu as pltpu
from jax.sharding import Mesh
from jax.sharding import PartitionSpec as P

HD = 128
SPAN = 64
NBT = 128
NEIGH = 2
STEP_SPANS = 2

LOW = jnp.bfloat16
F32 = jnp.float32


def dot_nt(a, b):
    return lax.dot_general(a, b, (((1,), (1,)), ((), ())), preferred_element_type=F32)


def dot_tn(a, b):
    return lax.dot_general(a, b, (((0,), (0,)), ((), ())), preferred_element_type=F32)


def dot_nn(a, b):
    return lax.dot_general(a, b, (((1,), (0,)), ((), ())), preferred_element_type=F32)


def attention_kernel(heads, owners, ids, place, q_ref, g_ref, k_ref, v_ref, dq_ref, store_ref, total):
    step = pl.program_id(0)
    factor = 1.0 / math.sqrt(HD)
    width = heads * HD
    me = lax.axis_index("enc")

    @pl.when(step == 0)
    def _():
        total[...] = jnp.zeros_like(total)

    for s in range(STEP_SPANS):
        span = step * STEP_SPANS + s
        slots = []
        for j in range(NEIGH):
            entry = place[0, ids[span, j]]
            away = jnp.where(me % 2 == 0, entry // 2 - me, me - entry // 2)
            slots.append(lax.rem(away + owners, owners) * 2 + entry % 2)
        for h in range(heads):
            cols = slice(h * HD, (h + 1) * HD)
            rows = slice(s * SPAN, (s + 1) * SPAN)
            q = q_ref[rows, cols]
            g = g_ref[rows, cols]
            k = k_ref[s * NEIGH : (s + 1) * NEIGH, :, cols].reshape(NEIGH * NBT, HD)
            v = v_ref[s * NEIGH : (s + 1) * NEIGH, :, cols].reshape(NEIGH * NBT, HD)
            scores = dot_nt(q, k) * factor
            weight_grad = dot_nt(g, v)
            exponent = jnp.exp(scores - jnp.max(scores, axis=1, keepdims=True))
            weights = exponent * (1.0 / jnp.sum(exponent, axis=1, keepdims=True))
            weights_low = weights.astype(LOW)
            delta = jnp.sum(weights_low.astype(F32) * weight_grad, axis=1, keepdims=True)
            score_low = (weights * (weight_grad - delta)).astype(LOW)
            dq_ref[rows, cols] = (dot_nn(score_low, k) * factor).astype(LOW)
            key_grad = dot_tn(score_low, q)
            value_grad = dot_tn(weights_low, g)
            for j in range(NEIGH):
                part = slice(j * NBT, (j + 1) * NBT)
                total[slots[j], :, cols] += key_grad[part]
                total[slots[j], :, width + h * HD : width + (h + 1) * HD] += value_grad[part]

    @pl.when(step == pl.num_programs(0) - 1)
    def _():
        store_ref[:, :, :width] = (total[:, :, :width] * factor).astype(LOW)
        store_ref[:, :, width:] = total[:, :, width:].astype(LOW)


def attention(queries, out_grad, keys, values, ids, place, owners):
    tokens, width = queries.shape
    slots = keys.shape[0]
    entries = place.shape[1]
    steps = slots // (NEIGH * STEP_SPANS)
    row_spec = pl.BlockSpec((STEP_SPANS * SPAN, width), lambda i: (i, 0))
    slot_spec = pl.BlockSpec((STEP_SPANS * NEIGH, NBT, width), lambda i: (i, 0, 0))
    scalars = pl.BlockSpec(memory_space=pltpu.SMEM)

    def kernel(*refs):
        attention_kernel(width // HD, owners, *refs)

    return pl.pallas_call(
        kernel,
        grid=(steps,),
        in_specs=[scalars, scalars, row_spec, row_spec, slot_spec, slot_spec],
        out_specs=[row_spec, pl.BlockSpec((entries, NBT, 2 * width), lambda i: (0, 0, 0))],
        out_shape=[
            jax.ShapeDtypeStruct((tokens, width), LOW),
            jax.ShapeDtypeStruct((entries, NBT, 2 * width), LOW),
        ],
        scratch_shapes=[pltpu.VMEM((entries, NBT, 2 * width), F32)],
        compiler_params=pltpu.CompilerParams(
            dimension_semantics=("arbitrary",), vmem_limit_bytes=56 * 1024 * 1024
        ),
        cost_estimate=pl.CostEstimate(flops=10**9, bytes_accessed=6 * 10**6, transcendentals=2 * 10**6),
        name="attention_back",
    )(ids, place, queries, out_grad, keys, values)


def copies_for(mine, sources):
    return jnp.broadcast_to(mine[None], (sources,) + mine.shape)


def exchange(copies):
    return lax.all_to_all(copies, ("dp", "sx"), split_axis=0, concat_axis=0, tiled=True)


def all_rows(same):
    sources, rows, depth = same.shape
    other = lax.ppermute(same, "core", [(0, 1), (1, 0)])
    first = lax.axis_index("core") == 0
    low = jnp.where(first, same, other)
    high = jnp.where(first, other, same)
    return jnp.stack([low, high], axis=1).reshape(sources * 2 * rows, depth)


def project_kernel(store_ref, weight_ref, out_ref):
    cap, tokens, depth = store_ref.shape
    raw = store_ref[...].reshape(cap * tokens, depth)
    out_ref[0] = dot_nt(raw, weight_ref[...]).astype(LOW)


def project(store, weight, first, owners):
    entries, tokens, depth = store.shape
    cap = entries // owners
    columns = weight.shape[0]
    return pl.pallas_call(
        project_kernel,
        grid=(owners - 1,),
        in_specs=[
            pl.BlockSpec((cap, tokens, depth), lambda i: (lax.rem(i + first, owners), 0, 0)),
            pl.BlockSpec((columns, depth), lambda i: (0, 0)),
        ],
        out_specs=pl.BlockSpec((1, cap * tokens, columns), lambda i: (i, 0, 0)),
        out_shape=jax.ShapeDtypeStruct((owners - 1, cap * tokens, columns), LOW),
        compiler_params=pltpu.CompilerParams(
            dimension_semantics=("arbitrary",), vmem_limit_bytes=16 * 1024 * 1024
        ),
        cost_estimate=pl.CostEstimate(flops=8 * 10**9, bytes_accessed=3 * 10**7, transcendentals=0),
        name="project",
    )(store, weight)


def add_low(a, b):
    return (a.astype(F32) + b.astype(F32)).astype(LOW)


def local(queries, out_grad, keys, values, neighbour_ids, neighbour_place, kv_weight):
    owners = lax.axis_size("enc")
    dp_count, x_count = lax.axis_size("dp"), lax.axis_size("sx")
    rows = kv_weight.shape[1]
    depth = 2 * kv_weight.shape[2]
    half = owners // 2
    even = [(i, i ^ 1) for i in range(owners)]
    odd = [(i, (i + 1) % owners if i % 2 else (i - 1) % owners) for i in range(owners)]

    sources = dp_count * x_count

    mine = jnp.transpose(kv_weight, (1, 0, 2)).reshape(rows, depth)
    same = exchange(copies_for(mine, sources))
    query_grad, store = attention(
        queries, out_grad, keys, values, neighbour_ids, neighbour_place, owners
    )
    cap = store.shape[0] // owners
    same, store = lax.optimization_barrier((same, store))
    weight = all_rows(same)

    far = dot_nt(store[half * cap : (half + 1) * cap].reshape(cap * NBT, depth), weight).astype(LOW)
    far, weight = lax.optimization_barrier((far, weight))
    part = project(store, weight, half + 1, owners)

    def on_even(x):
        return lax.ppermute(x, "enc", even)

    def on_odd(x):
        return lax.ppermute(x, "enc", odd)

    cut = cap * NBT // 2
    a, b = on_even(far[:cut]), on_odd(far[cut:])
    forth, back = part[owners - 2], part[0]
    forth = jnp.concatenate([forth[:cut], add_low(forth[cut:], b)], axis=0)
    back = jnp.concatenate([add_low(back[:cut], a), back[cut:]], axis=0)
    a, b = on_even(forth), on_odd(back)
    for j in range(half - 2, 0, -1):
        a, b = (
            on_even(add_low(b, part[half - 1 + j])),
            on_odd(add_low(a, part[half - 1 - j])),
        )
    encoded = part[half - 1].astype(F32) + a.astype(F32) + b.astype(F32)
    return (query_grad, encoded.astype(LOW).reshape(cap, NBT, -1))


def solution(mesh):
    devices = mesh.devices
    dp_count, seq_count, enc_count = devices.shape
    split = Mesh(
        devices.reshape(dp_count, seq_count // 2, 2, enc_count), ("dp", "sx", "core", "enc")
    )
    group = ("dp", "sx", "core")
    placed = (
        P(group, "enc"),
        P(group, "enc"),
        P(group, None, "enc"),
        P(group, None, "enc"),
        P(group, None),
        P(group, None),
        P(None, group, "enc"),
    )
    return jax.shard_map(
        local,
        mesh=split,
        in_specs=placed,
        out_specs=(P(group, "enc"), P(("dp", "sx", "core", "enc"), None, None)),
        check_vma=False,
    )
```

```python
import math

import jax
import jax.numpy as jnp
from jax import lax
from jax.experimental import pallas as pl
from jax.experimental.pallas import tpu as pltpu
from jax.sharding import Mesh
from jax.sharding import PartitionSpec as P

HD = 128
SPAN = 64
NBT = 128
NEIGH = 2
STEP_SPANS = 4

LOW = jnp.bfloat16
F32 = jnp.float32


def dot_nt(a, b):
    return lax.dot_general(a, b, (((1,), (1,)), ((), ())), preferred_element_type=F32)


def dot_tn(a, b):
    return lax.dot_general(a, b, (((0,), (0,)), ((), ())), preferred_element_type=F32)


def dot_nn(a, b):
    return lax.dot_general(a, b, (((1,), (0,)), ((), ())), preferred_element_type=F32)


def softmax_back(scores, weight_grad):
    exponent = jnp.exp(scores - jnp.max(scores, axis=1, keepdims=True))
    weights = exponent * (1.0 / jnp.sum(exponent, axis=1, keepdims=True))
    weights_low = weights.astype(LOW)
    delta = jnp.sum(weights_low.astype(F32) * weight_grad, axis=1, keepdims=True)
    return weights_low, (weights * (weight_grad - delta)).astype(LOW)


def attention_kernel(heads, owners, ids, place, q_ref, g_ref, k_ref, v_ref, dq_ref, store_ref, far_ref, total):
    step = pl.program_id(0)
    factor = 1.0 / math.sqrt(HD)
    width = heads * HD
    me = lax.axis_index("enc")

    @pl.when(step == 0)
    def _():
        total[...] = jnp.zeros_like(total)

    slots = []
    for s in range(STEP_SPANS):
        for j in range(NEIGH):
            entry = place[0, ids[j, step * STEP_SPANS + s]]
            away = jnp.where(me % 2 == 0, entry // 2 - me, me - entry // 2)
            slots.append(lax.rem(away + owners, owners) * 2 + entry % 2)

    def rows_of(ref, unit):
        s, h = unit
        return ref[s * SPAN : (s + 1) * SPAN, h * HD : (h + 1) * HD]

    def slots_of(ref, unit):
        s, h = unit
        block = ref[s * NEIGH : (s + 1) * NEIGH, :, h * HD : (h + 1) * HD]
        return block.reshape(NEIGH * NBT, HD)

    units = [(s, h) for s in range(STEP_SPANS) for h in range(heads)]
    scores = [dot_nt(rows_of(q_ref, u), slots_of(k_ref, u)) * factor for u in units]
    weight_grads = [dot_nt(rows_of(g_ref, u), slots_of(v_ref, u)) for u in units]
    lows = [softmax_back(a, b) for a, b in zip(scores, weight_grads)]
    for (s, h), (_, score_low) in zip(units, lows):
        dq = dot_nn(score_low, slots_of(k_ref, (s, h))) * factor
        dq_ref[s * SPAN : (s + 1) * SPAN, h * HD : (h + 1) * HD] = dq.astype(LOW)
    key_grads = [dot_tn(low[1], rows_of(q_ref, u)) for low, u in zip(lows, units)]
    value_grads = [dot_tn(low[0], rows_of(g_ref, u)) for low, u in zip(lows, units)]
    for (s, h), key_grad, value_grad in zip(units, key_grads, value_grads):
        for j in range(NEIGH):
            slot = slots[s * NEIGH + j]
            part = slice(j * NBT, (j + 1) * NBT)
            total[slot, :, h * HD : (h + 1) * HD] += key_grad[part]
            total[slot, :, width + h * HD : width + (h + 1) * HD] += value_grad[part]

    @pl.when(step == pl.num_programs(0) - 1)
    def _():
        store_ref[:, :, :width] = (total[:, :, :width] * factor).astype(LOW)
        store_ref[:, :, width:] = total[:, :, width:].astype(LOW)
        far_ref[...] = store_ref[pl.ds(store_ref.shape[0] // 2, far_ref.shape[0])]


def attention(queries, out_grad, keys, values, ids, place, owners):
    tokens, width = queries.shape
    slots = keys.shape[0]
    entries = place.shape[1]
    steps = slots // (NEIGH * STEP_SPANS)
    row_spec = pl.BlockSpec((STEP_SPANS * SPAN, width), lambda i: (i, 0))
    slot_spec = pl.BlockSpec((STEP_SPANS * NEIGH, NBT, width), lambda i: (i, 0, 0))
    scalars = pl.BlockSpec(memory_space=pltpu.SMEM)

    def whole_spec(count):
        return pl.BlockSpec((count, NBT, 2 * width), lambda i: (0, 0, 0))

    def kernel(*refs):
        attention_kernel(width // HD, owners, *refs)

    return pl.pallas_call(
        kernel,
        grid=(steps,),
        in_specs=[scalars, scalars, row_spec, row_spec, slot_spec, slot_spec],
        out_specs=[row_spec, whole_spec(entries), whole_spec(entries // owners)],
        out_shape=[
            jax.ShapeDtypeStruct((tokens, width), LOW),
            jax.ShapeDtypeStruct((entries, NBT, 2 * width), LOW),
            jax.ShapeDtypeStruct((entries // owners, NBT, 2 * width), LOW),
        ],
        scratch_shapes=[pltpu.VMEM((entries, NBT, 2 * width), F32)],
        compiler_params=pltpu.CompilerParams(
            dimension_semantics=("arbitrary",), vmem_limit_bytes=56 * 1024 * 1024
        ),
        cost_estimate=pl.CostEstimate(flops=10**9, bytes_accessed=6 * 10**6, transcendentals=2 * 10**6),
        name="attention_back",
    )(ids.T, place, queries, out_grad, keys, values)


def exchange(mine):
    sources = lax.axis_size("dp") * lax.axis_size("sx")
    copies = jnp.broadcast_to(mine[None], (sources,) + mine.shape)
    return lax.all_to_all(copies, ("dp", "sx"), split_axis=0, concat_axis=0, tiled=True)


def all_rows(same):
    sources, rows, depth = same.shape
    other = lax.ppermute(same, "core", [(0, 1), (1, 0)])
    first = lax.axis_index("core") == 0
    low = jnp.where(first, same, other)
    high = jnp.where(first, other, same)
    return jnp.stack([low, high], axis=1).reshape(sources * 2 * rows, depth)


def add_low(a, b):
    return (a.astype(F32) + b.astype(F32)).astype(LOW)


def local(queries, out_grad, keys, values, neighbour_ids, neighbour_place, kv_weight):
    owners = lax.axis_size("enc")
    rows = kv_weight.shape[1]
    half = owners // 2
    even = [(i, i ^ 1) for i in range(owners)]
    odd = [(i, (i + 1) % owners if i % 2 else (i - 1) % owners) for i in range(owners)]

    same = exchange(jnp.transpose(kv_weight, (1, 0, 2)).reshape(rows, -1))
    query_grad, store, far_store = attention(
        queries, out_grad, keys, values, neighbour_ids, neighbour_place, owners
    )
    cap = store.shape[0] // owners
    same, store, far_store = lax.optimization_barrier((same, store, far_store))
    weight = all_rows(same)

    def project(raw, weight):
        raw = raw.reshape(cap * NBT, -1)
        return lax.optimization_barrier(dot_nt(raw, weight).astype(LOW))

    def chunk(j):
        return store[j * cap : (j + 1) * cap]

    def on_even(x):
        return lax.ppermute(x, "enc", even)

    def on_odd(x):
        return lax.ppermute(x, "enc", odd)

    cut = cap * NBT // 2
    far = project(far_store, weight)
    a, b = on_even(far[:cut]), on_odd(far[cut:])
    back, forth = project(chunk(half + 1), weight), project(chunk(half - 1), weight)
    weight, _ = lax.optimization_barrier((weight, a))
    back = jnp.concatenate([add_low(back[:cut], a), back[cut:]], axis=0)
    forth = jnp.concatenate([forth[:cut], add_low(forth[cut:], b)], axis=0)
    a, b = on_even(forth), on_odd(back)
    for j in range(half - 2, 0, -1):
        forth, back = project(chunk(j), weight), project(chunk(owners - j), weight)
        a, b = on_even(add_low(b, forth)), on_odd(add_low(a, back))
    own = project(chunk(0), weight)
    encoded = own.astype(F32) + a.astype(F32) + b.astype(F32)
    return (query_grad, encoded.astype(LOW).reshape(cap, NBT, -1))


def solution(mesh):
    devices = mesh.devices
    dp_count, seq_count, enc_count = devices.shape
    split = Mesh(
        devices.reshape(dp_count, seq_count // 2, 2, enc_count), ("dp", "sx", "core", "enc")
    )
    group = ("dp", "sx", "core")
    placed = (
        P(group, "enc"),
        P(group, "enc"),
        P(group, None, "enc"),
        P(group, None, "enc"),
        P(group, None),
        P(group, None),
        P(None, group, "enc"),
    )
    return jax.shard_map(
        local,
        mesh=split,
        in_specs=placed,
        out_specs=(P(group, "enc"), P(("dp", "sx", "core", "enc"), None, None)),
        check_vma=False,
    )
```

```python
import math

import jax
import jax.numpy as jnp
from jax import lax
from jax.experimental import pallas as pl
from jax.experimental.pallas import tpu as pltpu
from jax.sharding import Mesh
from jax.sharding import PartitionSpec as P

HD = 128
SPAN = 64
NBT = 128
NEIGH = 2
STEP_SPANS = 4

LOW = jnp.bfloat16
F32 = jnp.float32


def dot_nt(a, b):
    return lax.dot_general(a, b, (((1,), (1,)), ((), ())), preferred_element_type=F32)


def dot_tn(a, b):
    return lax.dot_general(a, b, (((0,), (0,)), ((), ())), preferred_element_type=F32)


def dot_nn(a, b):
    return lax.dot_general(a, b, (((1,), (0,)), ((), ())), preferred_element_type=F32)


def softmax_back(scores, weight_grad):
    exponent = jnp.exp(scores - jnp.max(scores, axis=1, keepdims=True))
    weights = exponent * (1.0 / jnp.sum(exponent, axis=1, keepdims=True))
    weights_low = weights.astype(LOW)
    delta = jnp.sum(weights_low.astype(F32) * weight_grad, axis=1, keepdims=True)
    return weights_low, (weights * (weight_grad - delta)).astype(LOW)


def entry_place(me, entry, owners):
    owner = entry // 2
    pairs = owners // 2
    parity = owner % 2
    side = me % 2
    ahead = lax.rem(owner // 2 - me // 2 + pairs, pairs)
    near = (ahead == 1) | (ahead == pairs - 1)
    handler = jnp.where(near, jnp.where(ahead == 1, 1, 0), parity)
    slot = jnp.where(near, jnp.where(handler == parity, 2, 1), jnp.where(ahead == 0, 3, 0))
    return (jnp.where(handler == side, 0, pairs) + slot) * 2 + entry % 2


def attention_kernel(heads, owners, ids, place, q_ref, g_ref, k_ref, v_ref, dq_ref, kept_ref, *rest):
    *sent_refs, total = rest
    step = pl.program_id(0)
    factor = 1.0 / math.sqrt(HD)
    width = heads * HD
    me = lax.axis_index("pair") * 2 + lax.axis_index("side")

    @pl.when(step == 0)
    def _():
        total[...] = jnp.zeros_like(total)

    slots = []
    for s in range(STEP_SPANS):
        for j in range(NEIGH):
            entry = place[0, ids[j, step * STEP_SPANS + s]]
            slots.append(entry_place(me, entry, owners))

    def rows_of(ref, unit):
        s, h = unit
        return ref[s * SPAN : (s + 1) * SPAN, h * HD : (h + 1) * HD]

    def slots_of(ref, unit):
        s, h = unit
        block = ref[s * NEIGH : (s + 1) * NEIGH, :, h * HD : (h + 1) * HD]
        return block.reshape(NEIGH * NBT, HD)

    units = [(s, h) for s in range(STEP_SPANS) for h in range(heads)]
    scores = [dot_nt(rows_of(q_ref, u), slots_of(k_ref, u)) * factor for u in units]
    weight_grads = [dot_nt(rows_of(g_ref, u), slots_of(v_ref, u)) for u in units]
    lows = [softmax_back(a, b) for a, b in zip(scores, weight_grads)]
    for (s, h), (_, score_low) in zip(units, lows):
        dq = dot_nn(score_low, slots_of(k_ref, (s, h))) * factor
        dq_ref[s * SPAN : (s + 1) * SPAN, h * HD : (h + 1) * HD] = dq.astype(LOW)
    key_grads = [dot_tn(low[1], rows_of(q_ref, u)) for low, u in zip(lows, units)]
    value_grads = [dot_tn(low[0], rows_of(g_ref, u)) for low, u in zip(lows, units)]
    for (s, h), key_grad, value_grad in zip(units, key_grads, value_grads):
        for j in range(NEIGH):
            slot = slots[s * NEIGH + j]
            part = slice(j * NBT, (j + 1) * NBT)
            total[slot, :, h * HD : (h + 1) * HD] += key_grad[part]
            total[slot, :, width + h * HD : width + (h + 1) * HD] += value_grad[part]

    @pl.when(step == pl.num_programs(0) - 1)
    def _():
        first = 0
        for ref in (kept_ref, *sent_refs):
            part = slice(first, first + ref.shape[0])
            ref[:, :, :width] = (total[part, :, :width] * factor).astype(LOW)
            ref[:, :, width:] = total[part, :, width:].astype(LOW)
            first += ref.shape[0]


def attention(queries, out_grad, keys, values, ids, place, owners):
    tokens, width = queries.shape
    slots = keys.shape[0]
    entries = place.shape[1]
    steps = slots // (NEIGH * STEP_SPANS)
    row_spec = pl.BlockSpec((STEP_SPANS * SPAN, width), lambda i: (i, 0))
    slot_spec = pl.BlockSpec((STEP_SPANS * NEIGH, NBT, width), lambda i: (i, 0, 0))
    scalars = pl.BlockSpec(memory_space=pltpu.SMEM)

    shapes = [(entries // 2, NBT, 2 * width)] * 2

    def kernel(*refs):
        attention_kernel(width // HD, owners, *refs)

    return pl.pallas_call(
        kernel,
        grid=(steps,),
        in_specs=[scalars, scalars, row_spec, row_spec, slot_spec, slot_spec],
        out_specs=[row_spec] + [pl.BlockSpec(shape, lambda i: (0, 0, 0)) for shape in shapes],
        out_shape=[jax.ShapeDtypeStruct((tokens, width), LOW)]
        + [jax.ShapeDtypeStruct(shape, LOW) for shape in shapes],
        scratch_shapes=[pltpu.VMEM((entries, NBT, 2 * width), F32)],
        compiler_params=pltpu.CompilerParams(
            dimension_semantics=("arbitrary",), vmem_limit_bytes=56 * 1024 * 1024
        ),
        cost_estimate=pl.CostEstimate(flops=10**9, bytes_accessed=6 * 10**6, transcendentals=2 * 10**6),
        name="attention_back",
    )(ids.T, place, queries, out_grad, keys, values)


def exchange(mine, axes):
    sizes = tuple(lax.axis_size(axis) for axis in axes)
    copies = jnp.broadcast_to(mine[None], (math.prod(sizes),) + mine.shape)
    theirs = lax.all_to_all(copies, axes, split_axis=0, concat_axis=0, tiled=True)
    return theirs.reshape(sizes + mine.shape)


def column_order(rows):
    x_count, dp_count = lax.axis_size("sx"), lax.axis_size("dp")
    count = 2 * x_count * dp_count * rows
    at = jnp.arange(count, dtype=jnp.int32)
    row = at % rows
    dp = at // rows % dp_count
    x = at // (rows * dp_count) % x_count
    core = (at // (rows * dp_count * x_count) + lax.axis_index("core")) % 2
    column = ((dp * x_count + x) * 2 + core) * rows + row
    return (column[:, None] == at[None, :]).astype(LOW)


def add_low(a, b):
    return (a.astype(F32) + b.astype(F32)).astype(LOW)


def local(queries, out_grad, keys, values, neighbour_ids, neighbour_place, kv_weight):
    ring = ("pair", "side")
    owners = lax.axis_size("pair") * 2
    rows = kv_weight.shape[1]
    pair = [(i, i ^ 1) for i in range(owners)]
    near = [(i, (i + 1) % owners if i % 2 else (i - 1) % owners) for i in range(owners)]
    next_pair = [(i, (i + 2) % owners if i % 2 else (i - 2) % owners) for i in range(owners)]

    mine = jnp.transpose(kv_weight, (1, 0, 2)).reshape(rows, -1)
    along_dp = exchange(mine, ("dp", "side"))
    query_grad, kept, sent = attention(
        queries, out_grad, keys, values, neighbour_ids, neighbour_place, owners
    )
    received = lax.ppermute(sent, ring, pair)
    along_dp, kept = lax.optimization_barrier((along_dp, kept))
    same = exchange(along_dp, ("sx",))
    order = column_order(rows)
    same, order = lax.optimization_barrier((same, order))

    here = jnp.swapaxes(same, 2, 3).reshape(-1, 2 * mine.shape[1])
    weight = jnp.concatenate([here, lax.ppermute(here, "core", [(0, 1), (1, 0)])])

    left = lax.axis_index("side") == 0
    heads = [jnp.where(left, kept, received), jnp.where(left, received, kept)]
    raw = jnp.concatenate(heads, axis=2)
    raw = raw.reshape(owners // 2, -1, raw.shape[2])
    cap = kept.shape[0] * 2 // owners

    def project(chunk):
        return lax.optimization_barrier(dot_nt(chunk, weight).astype(LOW))

    opposite = lax.ppermute(project(raw[0]), ring, next_pair)
    other = lax.ppermute(project(raw[1]), ring, near)
    last = lax.ppermute(add_low(project(raw[2]), opposite), ring, next_pair)
    encoded = project(raw[3]).astype(F32) + other.astype(F32) + last.astype(F32)
    encoded = dot_nn(encoded.astype(LOW), order).astype(LOW)
    return (query_grad, encoded.reshape(cap, NBT, -1))


def solution(mesh):
    devices = mesh.devices
    dp_count, seq_count, enc_count = devices.shape
    split = Mesh(
        devices.reshape(dp_count, seq_count // 2, 2, enc_count // 2, 2),
        ("dp", "sx", "core", "pair", "side"),
    )
    group = ("dp", "sx", "core")
    ring = ("pair", "side")
    placed = (
        P(group, ring),
        P(group, ring),
        P(group, None, ring),
        P(group, None, ring),
        P(group, None),
        P(group, None),
        P(None, group, ring),
    )
    return jax.shard_map(
        local,
        mesh=split,
        in_specs=placed,
        out_specs=(P(group, ring), P(group + ring, None, None)),
        check_vma=False,
    )
```

```python
import math

import jax
import jax.numpy as jnp
from jax import lax
from jax.experimental import pallas as pl
from jax.experimental.pallas import tpu as pltpu
from jax.sharding import Mesh
from jax.sharding import PartitionSpec as P

HD = 128
SPAN = 64
NBT = 128
NEIGH = 2
STEP_SPANS = 8

LOW = jnp.bfloat16
F32 = jnp.float32


def dot_nt(a, b):
    return lax.dot_general(a, b, (((1,), (1,)), ((), ())), preferred_element_type=F32)


def dot_tn(a, b):
    return lax.dot_general(a, b, (((0,), (0,)), ((), ())), preferred_element_type=F32)


def dot_nn(a, b):
    return lax.dot_general(a, b, (((1,), (0,)), ((), ())), preferred_element_type=F32)


def softmax_back(scores, weight_grad):
    exponent = jnp.exp(scores - jnp.max(scores, axis=1, keepdims=True))
    weights = exponent * (1.0 / jnp.sum(exponent, axis=1, keepdims=True))
    weights_low = weights.astype(LOW)
    delta = jnp.sum(weights_low.astype(F32) * weight_grad, axis=1, keepdims=True)
    return weights_low, (weights * (weight_grad - delta)).astype(LOW)


def entry_place(me, entry, owners):
    owner = entry // 2
    pairs = owners // 2
    parity = owner % 2
    side = me % 2
    ahead = lax.rem(owner // 2 - me // 2 + pairs, pairs)
    near = (ahead == 1) | (ahead == pairs - 1)
    handler = jnp.where(near, jnp.where(ahead == 1, 1, 0), parity)
    slot = jnp.where(near, jnp.where(handler == parity, 2, 1), jnp.where(ahead == 0, 3, 0))
    return (jnp.where(handler == side, 0, pairs) + slot) * 2 + entry % 2


def attention_kernel(heads, owners, ids, place, q_ref, g_ref, k_ref, v_ref, dq_ref, kept_ref, *rest):
    *sent_refs, total = rest
    factor = 1.0 / math.sqrt(HD)
    width = heads * HD
    me = lax.axis_index("pair") * 2 + lax.axis_index("side")

    total[...] = jnp.zeros_like(total)

    slots = []
    for s in range(STEP_SPANS):
        for j in range(NEIGH):
            entry = place[0, ids[j, s]]
            slots.append(entry_place(me, entry, owners))

    def rows_of(ref, unit):
        s, h = unit
        return ref[s * SPAN : (s + 1) * SPAN, h * HD : (h + 1) * HD]

    def slots_of(ref, unit):
        s, h = unit
        block = ref[s * NEIGH : (s + 1) * NEIGH, :, h * HD : (h + 1) * HD]
        return block.reshape(NEIGH * NBT, HD)

    units = [(s, h) for s in range(STEP_SPANS) for h in range(heads)]
    scores = [dot_nt(rows_of(q_ref, u), slots_of(k_ref, u)) * factor for u in units]
    weight_grads = [dot_nt(rows_of(g_ref, u), slots_of(v_ref, u)) for u in units]
    lows = [softmax_back(a, b) for a, b in zip(scores, weight_grads)]
    for (s, h), (_, score_low) in zip(units, lows):
        dq = dot_nn(score_low, slots_of(k_ref, (s, h))) * factor
        dq_ref[s * SPAN : (s + 1) * SPAN, h * HD : (h + 1) * HD] = dq.astype(LOW)
    key_grads = [dot_tn(low[1], rows_of(q_ref, u)) for low, u in zip(lows, units)]
    value_grads = [dot_tn(low[0], rows_of(g_ref, u)) for low, u in zip(lows, units)]
    for (s, h), key_grad, value_grad in zip(units, key_grads, value_grads):
        for j in range(NEIGH):
            slot = slots[s * NEIGH + j]
            part = slice(j * NBT, (j + 1) * NBT)
            total[slot, :, h * HD : (h + 1) * HD] += key_grad[part]
            total[slot, :, width + h * HD : width + (h + 1) * HD] += value_grad[part]

    first = 0
    for ref in (kept_ref, *sent_refs):
        part = slice(first, first + ref.shape[0])
        ref[:, :, :width] = (total[part, :, :width] * factor).astype(LOW)
        ref[:, :, width:] = total[part, :, width:].astype(LOW)
        first += ref.shape[0]


def attention(queries, out_grad, keys, values, ids, place, owners):
    tokens, width = queries.shape
    slots = keys.shape[0]
    entries = place.shape[1]
    cap = entries // owners
    steps = slots // (NEIGH * STEP_SPANS)
    row_spec = pl.BlockSpec((STEP_SPANS * SPAN, width), lambda i: (i, 0))
    slot_spec = pl.BlockSpec((STEP_SPANS * NEIGH, NBT, width), lambda i: (i, 0, 0))
    scalars = pl.BlockSpec(memory_space=pltpu.SMEM)

    shapes = [(n, NBT, 2 * width) for n in (entries // 2, entries // 2 - cap, cap)]

    def kernel(*refs):
        attention_kernel(width // HD, owners, *refs)

    return pl.pallas_call(
        kernel,
        grid=(steps,),
        in_specs=[scalars, scalars, row_spec, row_spec, slot_spec, slot_spec],
        out_specs=[row_spec] + [pl.BlockSpec(shape, lambda i: (0, 0, 0)) for shape in shapes],
        out_shape=[jax.ShapeDtypeStruct((tokens, width), LOW)]
        + [jax.ShapeDtypeStruct(shape, LOW) for shape in shapes],
        scratch_shapes=[pltpu.VMEM((entries, NBT, 2 * width), F32)],
        compiler_params=pltpu.CompilerParams(
            dimension_semantics=("arbitrary",), vmem_limit_bytes=56 * 1024 * 1024
        ),
        cost_estimate=pl.CostEstimate(flops=10**9, bytes_accessed=6 * 10**6, transcendentals=2 * 10**6),
        name="attention_back",
    )(ids.T, place, queries, out_grad, keys, values)


def exchange(mine, axes):
    sizes = tuple(lax.axis_size(axis) for axis in axes)
    copies = jnp.broadcast_to(mine[None], (math.prod(sizes),) + mine.shape)
    theirs = lax.all_to_all(copies, axes, split_axis=0, concat_axis=0, tiled=True)
    return theirs.reshape(sizes + mine.shape)


def column_order(rows):
    x_count, dp_count = lax.axis_size("sx"), lax.axis_size("dp")
    count = 2 * x_count * dp_count * rows
    at = jnp.arange(count, dtype=jnp.int32)
    row = at % rows
    dp = at // rows % dp_count
    x = at // (rows * dp_count) % x_count
    core = (at // (rows * dp_count * x_count) + lax.axis_index("core")) % 2
    column = ((dp * x_count + x) * 2 + core) * rows + row
    return (column[:, None] == at[None, :]).astype(LOW)


def add_low(a, b):
    return (a.astype(F32) + b.astype(F32)).astype(LOW)


def local(queries, out_grad, keys, values, neighbour_ids, neighbour_place, kv_weight):
    ring = ("pair", "side")
    owners = lax.axis_size("pair") * 2
    rows = kv_weight.shape[1]
    pair = [(i, i ^ 1) for i in range(owners)]
    near = [(i, (i + 1) % owners if i % 2 else (i - 1) % owners) for i in range(owners)]
    next_pair = [(i, (i + 2) % owners if i % 2 else (i - 2) % owners) for i in range(owners)]

    mine = jnp.transpose(kv_weight, (1, 0, 2)).reshape(rows, -1)
    along_dp = exchange(mine, ("dp", "side"))
    query_grad, kept, sent, sent_own = attention(
        queries, out_grad, keys, values, neighbour_ids, neighbour_place, owners
    )
    received = lax.ppermute(sent, ring, pair)
    along_dp, kept = lax.optimization_barrier((along_dp, kept))
    same = exchange(along_dp, ("sx",))
    order = column_order(rows)
    same, order, received = lax.optimization_barrier((same, order, received))

    here = jnp.swapaxes(same, 2, 3).reshape(-1, 2 * mine.shape[1])
    weight = jnp.concatenate([here, lax.ppermute(here, "core", [(0, 1), (1, 0)])])

    left = lax.axis_index("side") == 0
    cap = sent_own.shape[0]

    def both_heads(mine, theirs):
        heads = [jnp.where(left, mine, theirs), jnp.where(left, theirs, mine)]
        raw = jnp.concatenate(heads, axis=2)
        return raw.reshape(-1, cap * NBT, raw.shape[2])

    raw = both_heads(kept[:-cap], received)

    def project(chunk):
        return lax.optimization_barrier(dot_nt(chunk, weight).astype(LOW))

    part = project(raw[0])
    opposite = lax.ppermute(part, ring, next_pair)
    other = lax.ppermute(project(raw[1]), ring, near)
    sent_own, _ = lax.optimization_barrier((sent_own, part))
    own = both_heads(kept[-cap:], lax.ppermute(sent_own, ring, pair))[0]
    last = lax.ppermute(add_low(project(raw[2]), opposite), ring, next_pair)
    encoded = project(own).astype(F32) + other.astype(F32) + last.astype(F32)
    encoded = dot_nn(encoded.astype(LOW), order).astype(LOW)
    return (query_grad, encoded.reshape(cap, NBT, -1))


def solution(mesh):
    devices = mesh.devices
    dp_count, seq_count, enc_count = devices.shape
    split = Mesh(
        devices.reshape(dp_count, seq_count // 2, 2, enc_count // 2, 2),
        ("dp", "sx", "core", "pair", "side"),
    )
    group = ("dp", "sx", "core")
    ring = ("pair", "side")
    placed = (
        P(group, ring),
        P(group, ring),
        P(group, None, ring),
        P(group, None, ring),
        P(group, None),
        P(group, None),
        P(None, group, ring),
    )
    return jax.shard_map(
        local,
        mesh=split,
        in_specs=placed,
        out_specs=(P(group, ring), P(group + ring, None, None)),
        check_vma=False,
    )
```

```python
import math

import jax
import jax.numpy as jnp
from jax import lax
from jax.experimental import pallas as pl
from jax.experimental.pallas import tpu as pltpu
from jax.sharding import Mesh
from jax.sharding import PartitionSpec as P

HD = 128
SPAN = 64
NBT = 128
NEIGH = 2
STEP_SPANS = 4

LOW = jnp.bfloat16
F32 = jnp.float32


def dot_nt(a, b):
    return lax.dot_general(a, b, (((1,), (1,)), ((), ())), preferred_element_type=F32)


def dot_tn(a, b):
    return lax.dot_general(a, b, (((0,), (0,)), ((), ())), preferred_element_type=F32)


def dot_nn(a, b):
    return lax.dot_general(a, b, (((1,), (0,)), ((), ())), preferred_element_type=F32)


def softmax_back(scores, weight_grad):
    exponent = jnp.exp(scores - jnp.max(scores, axis=1, keepdims=True))
    weights = exponent * (1.0 / jnp.sum(exponent, axis=1, keepdims=True))
    weights_low = weights.astype(LOW)
    delta = jnp.sum(weights_low.astype(F32) * weight_grad, axis=1, keepdims=True)
    return weights_low, (weights * (weight_grad - delta)).astype(LOW)


def entry_place(me, entry, owners):
    owner = entry // 2
    pairs = owners // 2
    parity = owner % 2
    side = me % 2
    ahead = lax.rem(owner // 2 - me // 2 + pairs, pairs)
    near = (ahead == 1) | (ahead == pairs - 1)
    handler = jnp.where(near, jnp.where(ahead == 1, 1, 0), parity)
    slot = jnp.where(near, jnp.where(handler == parity, 2, 1), jnp.where(ahead == 0, 3, 0))
    return (jnp.where(handler == side, 0, pairs) + slot) * 2 + entry % 2


def attention_kernel(heads, owners, ids, place, q_ref, g_ref, k_ref, v_ref, dq_ref, kept_ref, *rest):
    *sent_refs, total = rest
    step = pl.program_id(0)
    factor = 1.0 / math.sqrt(HD)
    width = heads * HD
    me = lax.axis_index("pair") * 2 + lax.axis_index("side")

    @pl.when(step == 0)
    def _():
        total[...] = jnp.zeros_like(total)

    slots = []
    for s in range(STEP_SPANS):
        for j in range(NEIGH):
            entry = place[0, ids[j, step * STEP_SPANS + s]]
            slots.append(entry_place(me, entry, owners))

    def rows_of(ref, unit):
        s, h = unit
        return ref[s * SPAN : (s + 1) * SPAN, h * HD : (h + 1) * HD]

    def slots_of(ref, unit):
        s, h = unit
        block = ref[s * NEIGH : (s + 1) * NEIGH, :, h * HD : (h + 1) * HD]
        return block.reshape(NEIGH * NBT, HD)

    units = [(s, h) for s in range(STEP_SPANS) for h in range(heads)]
    scores = [dot_nt(rows_of(q_ref, u), slots_of(k_ref, u)) * factor for u in units]
    weight_grads = [dot_nt(rows_of(g_ref, u), slots_of(v_ref, u)) for u in units]
    lows = [softmax_back(a, b) for a, b in zip(scores, weight_grads)]
    for (s, h), (_, score_low) in zip(units, lows):
        dq = dot_nn(score_low, slots_of(k_ref, (s, h))) * factor
        dq_ref[s * SPAN : (s + 1) * SPAN, h * HD : (h + 1) * HD] = dq.astype(LOW)
    key_grads = [dot_tn(low[1], rows_of(q_ref, u)) for low, u in zip(lows, units)]
    value_grads = [dot_tn(low[0], rows_of(g_ref, u)) for low, u in zip(lows, units)]
    for (s, h), key_grad, value_grad in zip(units, key_grads, value_grads):
        for j in range(NEIGH):
            slot = slots[s * NEIGH + j]
            part = slice(j * NBT, (j + 1) * NBT)
            total[slot, :, h * HD : (h + 1) * HD] += key_grad[part]
            total[slot, :, width + h * HD : width + (h + 1) * HD] += value_grad[part]

    @pl.when(step == pl.num_programs(0) - 1)
    def _():
        first = 0
        for ref in (kept_ref, *sent_refs):
            part = slice(first, first + ref.shape[0])
            ref[:, :, :width] = (total[part, :, :width] * factor).astype(LOW)
            ref[:, :, width:] = total[part, :, width:].astype(LOW)
            first += ref.shape[0]


def attention(queries, out_grad, keys, values, ids, place, owners):
    tokens, width = queries.shape
    slots = keys.shape[0]
    entries = place.shape[1]
    steps = slots // (NEIGH * STEP_SPANS)
    row_spec = pl.BlockSpec((STEP_SPANS * SPAN, width), lambda i: (i, 0))
    slot_spec = pl.BlockSpec((STEP_SPANS * NEIGH, NBT, width), lambda i: (i, 0, 0))
    scalars = pl.BlockSpec(memory_space=pltpu.SMEM)

    shapes = [(entries // 2, NBT, 2 * width)] * 2

    def kernel(*refs):
        attention_kernel(width // HD, owners, *refs)

    return pl.pallas_call(
        kernel,
        grid=(steps,),
        in_specs=[scalars, scalars, row_spec, row_spec, slot_spec, slot_spec],
        out_specs=[row_spec] + [pl.BlockSpec(shape, lambda i: (0, 0, 0)) for shape in shapes],
        out_shape=[jax.ShapeDtypeStruct((tokens, width), LOW)]
        + [jax.ShapeDtypeStruct(shape, LOW) for shape in shapes],
        scratch_shapes=[pltpu.VMEM((entries, NBT, 2 * width), F32)],
        compiler_params=pltpu.CompilerParams(
            dimension_semantics=("arbitrary",), vmem_limit_bytes=56 * 1024 * 1024
        ),
        cost_estimate=pl.CostEstimate(flops=10**9, bytes_accessed=6 * 10**6, transcendentals=2 * 10**6),
        name="attention_back",
    )(ids.T, place, queries, out_grad, keys, values)


def exchange(mine, axes):
    sizes = tuple(lax.axis_size(axis) for axis in axes)
    copies = jnp.broadcast_to(mine[None], (math.prod(sizes),) + mine.shape)
    theirs = lax.all_to_all(copies, axes, split_axis=0, concat_axis=0, tiled=True)
    return theirs.reshape(sizes + mine.shape)


def column_order(rows):
    x_count, dp_count = lax.axis_size("sx"), lax.axis_size("dp")
    count = 2 * x_count * dp_count * rows
    at = jnp.arange(count, dtype=jnp.int32)
    row = at % rows
    dp = at // rows % dp_count
    x = at // (rows * dp_count) % x_count
    core = (at // (rows * dp_count * x_count) + lax.axis_index("core")) % 2
    column = ((dp * x_count + x) * 2 + core) * rows + row
    return (column[:, None] == at[None, :]).astype(LOW)


def add_low(a, b):
    return (a.astype(F32) + b.astype(F32)).astype(LOW)


def local(queries, out_grad, keys, values, neighbour_ids, neighbour_place, kv_weight):
    ring = ("pair", "side")
    owners = lax.axis_size("pair") * 2
    rows = kv_weight.shape[1]
    pair = [(i, i ^ 1) for i in range(owners)]
    near = [(i, (i + 1) % owners if i % 2 else (i - 1) % owners) for i in range(owners)]
    next_pair = [(i, (i + 2) % owners if i % 2 else (i - 2) % owners) for i in range(owners)]

    along_dp = exchange(kv_weight, ("dp", "side"))
    query_grad, kept, sent = attention(
        queries, out_grad, keys, values, neighbour_ids, neighbour_place, owners
    )
    received = lax.ppermute(sent, ring, pair)
    along_dp, kept = lax.optimization_barrier((along_dp, kept))
    same = exchange(along_dp, ("sx",))
    order = column_order(rows)
    same, order = lax.optimization_barrier((same, order))

    here = jnp.transpose(same, (0, 1, 4, 2, 3, 5)).reshape(-1, 4 * kv_weight.shape[2])
    weight = jnp.concatenate([here, lax.ppermute(here, "core", [(0, 1), (1, 0)])])

    left = lax.axis_index("side") == 0
    heads = [jnp.where(left, kept, received), jnp.where(left, received, kept)]
    raw = jnp.concatenate(heads, axis=2)
    raw = raw.reshape(owners // 2, -1, raw.shape[2])
    cap = kept.shape[0] * 2 // owners

    def project(chunk):
        return lax.optimization_barrier(dot_nt(chunk, weight).astype(LOW))

    opposite = lax.ppermute(project(raw[0]), ring, next_pair)
    other = lax.ppermute(project(raw[1]), ring, near)
    last = lax.ppermute(add_low(project(raw[2]), opposite), ring, next_pair)
    encoded = project(raw[3]).astype(F32) + other.astype(F32) + last.astype(F32)
    encoded = dot_nn(encoded.astype(LOW), order).astype(LOW)
    return (query_grad, encoded.reshape(cap, NBT, -1))


def solution(mesh):
    devices = mesh.devices
    dp_count, seq_count, enc_count = devices.shape
    split = Mesh(
        devices.reshape(dp_count, seq_count // 2, 2, enc_count // 2, 2),
        ("dp", "sx", "core", "pair", "side"),
    )
    group = ("dp", "sx", "core")
    ring = ("pair", "side")
    placed = (
        P(group, ring),
        P(group, ring),
        P(group, None, ring),
        P(group, None, ring),
        P(group, None),
        P(group, None),
        P(None, group, ring),
    )
    return jax.shard_map(
        local,
        mesh=split,
        in_specs=placed,
        out_specs=(P(group, ring), P(group + ring, None, None)),
        check_vma=False,
    )
```
